512 devices in a mesh: seq: 64 (over y_lo, z, core), head: 8 (over y_hi, x).
Axes of the slice: x: 4, y: 8 (y_hi: 2, y_lo: 4; y = y_hi * 4 + y_lo), z: 8, core: 2. Of those that a mesh axis runs over, the one named last changes fastest.
Arguments:
- layer_input: bfloat16 [8192, 2048], P('seq', 'head'), may hold values from -6 to 6
- w_input: bfloat16 [2048, 4096], P('seq', 'head'), may hold values from -0.125 to 0.125
- w_gate: bfloat16 [2048, 4096], P('seq', 'head'), may hold values from -0.125 to 0.125
- w_maps: bfloat16 [2048, 256], P('seq'), may hold values from -0.125 to 0.125
- w_step: bfloat16 [2048, 64], P('seq', 'head'), may hold values from -0.125 to 0.125
- step_bias: float32 [64], P('head'), may hold values from -6 to -3
- decay_log: float32 [64], P('head'), may hold values from -8 to 0
- skip_gain: float32 [64], P('head'), may hold values from 0.5 to 1.5
- conv_input: float32 [4, 4096], P(None, 'head'), may hold values from -3 to 3
- conv_maps: float32 [4, 256], replicated, may hold values from -3 to 3
- norm_gain: float32 [4096], P('head'), may hold values from 0.1 to 1.9
- w_out: bfloat16 [4096, 2048], P('head', 'seq'), may hold values from -0.09375 to 0.09375
Outputs:
- mixed: bfloat16 [8192, 2048], P('seq', 'head')
The draws below stay inside these ranges and needn't reach their ends.
All inputs are finite; a program needn't handle non-finite values.
Results may differ from the reference program's by a relative error of at most 0.015.
Values may be sent and summed in bfloat16 or wider, within the bound.
No kernel may reach another device: no remote copies, remote signals or barrier semaphores. Data moves between devices by JAX's collectives and lax.ppermute only.
A program may use at most 128 MiB of HBM per device.

```python
import jax
import jax.numpy as jnp
from jax import lax

D = 2048
HEADS = 64
HEAD_DIM = 64
STATE = 128
SPAN = 128
CONV = 4
GROUP_HEADS = 8
INNER = 4096
TOKENS = 8192


def block_levels(key, dims, cuts, least, top_value):
    factor_of, own = 1.0, jax.random.fold_in(key, 6)
    for position, shards_of in cuts:
        heights = jnp.exp(jax.random.uniform(jax.random.fold_in(own, position), (shards_of,), jnp.float32, least / len(cuts), top_value / len(cuts)))
        factor_of = factor_of * jnp.repeat(heights, dims[position] // shards_of).reshape([-1 if axis == position else 1 for axis in range(len(dims))])
    return factor_of


def bell_draw(own_key, dims, scale, most, shards=(), dtype=jnp.bfloat16):
    result = scale * jax.random.normal(own_key, dims, jnp.float32)
    if shards:
        result = result * block_levels(own_key, dims, shards, -0.22, 0.18)
    return jnp.clip(result, -most, most).astype(dtype)


def setup_inputs(seed: int = 0) -> dict:
    streams_of = jax.random.split(jax.random.key(seed), 13)
    return {
        "layer_input": bell_draw(streams_of[0], (TOKENS, D), 1.0, 6.0, ((0, 64), (1, 8))),
        "w_input": bell_draw(streams_of[1], (D, INNER), D ** -0.5, 0.125, ((0, 64), (1, 8))),
        "w_gate": bell_draw(streams_of[2], (D, INNER), D ** -0.5, 0.125, ((0, 64), (1, 8))),
        "w_maps": bell_draw(streams_of[3], (D, 2 * STATE), D ** -0.5, 0.125, ((0, 64),)),
        "w_step": bell_draw(streams_of[4], (D, HEADS), D ** -0.5, 0.125, ((0, 64), (1, 8))),
        "step_bias": jnp.clip(-6.0 + 3.0 * jax.random.uniform(streams_of[5], (HEADS,), jnp.float32) ** block_levels(streams_of[5], (HEADS,), ((0, 8),), -0.2, 0.2), -6.0, -3.0),
        "decay_log": jnp.clip(-8.0 + 8.0 * jax.random.uniform(streams_of[6], (HEADS,), jnp.float32) ** block_levels(streams_of[6], (HEADS,), ((0, 8),), -0.2, 0.2), -8.0, 0.0),
        "skip_gain": jnp.clip(0.5 + 1.0 * jax.random.uniform(streams_of[7], (HEADS,), jnp.float32) ** block_levels(streams_of[7], (HEADS,), ((0, 8),), -0.2, 0.2), 0.5, 1.5),
        "conv_input": bell_draw(streams_of[8], (CONV, INNER), 0.5, 3.0, ((1, 8),), jnp.float32),
        "conv_maps": bell_draw(streams_of[9], (CONV, 2 * STATE), 0.5, 3.0, (), jnp.float32),
        "norm_gain": jnp.clip(1.0 + 0.18 * jax.random.normal(streams_of[10], (INNER,), jnp.float32), 0.1, 1.9),
        "w_out": bell_draw(streams_of[11], (INNER, D), INNER ** -0.5, 0.09375, ((0, 8), (1, 64))),
    }


def block_step(state, pieces):
    input_block, inmap_block, outmap_block, step_block, rate_block, skip_value = pieces
    cumulated = jnp.cumsum(rate_block, axis=0)
    scores = jnp.dot(outmap_block, inmap_block.T, preferred_element_type=jnp.float32)
    cum_heads = cumulated.T
    differ = cum_heads[:, :, None] - cum_heads[:, None, :]
    lower_mask = lax.broadcasted_iota(jnp.int32, scores.shape, 0) >= lax.broadcasted_iota(jnp.int32, scores.shape, 1)
    decay_mat = jnp.where(lower_mask, jnp.exp(jnp.where(lower_mask, differ, 0.0)), 0.0)
    weights_m = (scores[None] * decay_mat * step_block.T[:, None, :]).astype(jnp.bfloat16)
    input_float = input_block.astype(jnp.float32)
    inner_out = jnp.einsum('hls,shp->lhp', weights_m.astype(jnp.float32), input_float)
    end_weight = jnp.exp(cumulated[-1:] - cumulated) * step_block
    input_weighted = (input_float * end_weight[:, :, None]).astype(jnp.bfloat16)
    block_state = jnp.einsum('shp,sn->hpn', input_weighted.astype(jnp.float32), inmap_block.astype(jnp.float32))
    state_out = jnp.einsum('ln,hpn->lhp', outmap_block.astype(jnp.float32), state, precision=lax.Precision.HIGHEST) * jnp.exp(cumulated)[:, :, None]
    ssd_out = inner_out + state_out + skip_value[:, None] * input_float
    new_state = jnp.exp(cumulated[-1])[:, None, None] * state + block_state
    return (new_state, ssd_out)

def mixer(stream, w_input, w_gate, w_maps, w_step, step_bias, decay_log, skip_gain, conv_input, conv_maps, norm_gain):
    seq_len = stream.shape[0]
    proj_x = jnp.dot(stream, w_input, preferred_element_type=jnp.float32).astype(jnp.bfloat16)
    proj_z = jnp.dot(stream, w_gate, preferred_element_type=jnp.float32).astype(jnp.bfloat16)
    proj_bc = jnp.dot(stream, w_maps, preferred_element_type=jnp.float32).astype(jnp.bfloat16)
    proj_dt = jnp.dot(stream, w_step, preferred_element_type=jnp.float32)
    joined = jnp.concatenate([proj_x, proj_bc], 1).astype(jnp.float32)
    padded = jnp.concatenate([jnp.zeros((CONV - 1, joined.shape[1]), jnp.float32), joined], 0)
    tap_table = jnp.concatenate([conv_input, conv_maps], 1)
    running = tap_table[0] * padded[0:seq_len]
    for tap_index in range(1, CONV):
        running = running + tap_table[tap_index] * padded[tap_index:tap_index + seq_len]
    convolved = jax.nn.silu(running).astype(jnp.bfloat16)
    step_size = jax.nn.softplus(proj_dt + step_bias)
    decay_rate = step_size * -jnp.exp(decay_log)
    blocks = seq_len // SPAN
    x_heads = convolved[:, :INNER].reshape(blocks, SPAN, HEADS, HEAD_DIM)
    in_maps = convolved[:, INNER:INNER + STATE].reshape(blocks, SPAN, STATE)
    out_maps = convolved[:, INNER + STATE:].reshape(blocks, SPAN, STATE)
    step_blocks = step_size.reshape(blocks, SPAN, HEADS)
    rate_blocks = decay_rate.reshape(blocks, SPAN, HEADS)
    skip_rows = jnp.broadcast_to(skip_gain, (blocks, HEADS))
    start_state = jnp.zeros((HEADS, HEAD_DIM, STATE), jnp.float32)
    final_state, ssd_blocks = lax.scan(block_step, start_state, (x_heads, in_maps, out_maps, step_blocks, rate_blocks, skip_rows))
    ssd_full = ssd_blocks.reshape(seq_len, INNER)
    gated_out = ssd_full * jax.nn.silu(proj_z.astype(jnp.float32))
    grouped = gated_out.reshape(seq_len, -1, GROUP_HEADS * HEAD_DIM)
    mean_square = lax.optimization_barrier(jnp.mean(grouped * grouped, axis=-1, keepdims=True))
    normed = (grouped * lax.rsqrt(mean_square + 1e-05)).reshape(seq_len, INNER)
    return (normed * norm_gain).astype(jnp.bfloat16)

def reference(layer_input, w_input, w_gate, w_maps, w_step, step_bias, decay_log, skip_gain, conv_input, conv_maps, norm_gain, w_out):
    param_list = (w_input, w_gate, w_maps, w_step, step_bias, decay_log, skip_gain, conv_input, conv_maps, norm_gain)
    forward_mix = mixer(layer_input, *param_list)
    mirror_mix = mixer(layer_input[::-1, ::-1], *param_list)
    forward_term = jnp.dot(forward_mix, w_out, preferred_element_type=jnp.float32)
    mirror_term = jnp.dot(mirror_mix, w_out, preferred_element_type=jnp.float32)
    return (forward_term + mirror_term[::-1, ::-1]).astype(jnp.bfloat16)
```

```python
import jax
import jax.numpy as jnp
from jax import lax
from jax.experimental import pallas as pl
from jax.experimental.pallas import tpu as pltpu
from jax.sharding import Mesh
from jax.sharding import PartitionSpec as P

HEAD_DIM = 64
SPAN = 128
CONV = 4
STATE = 128
HALO = 16
EXT = SPAN + HALO
AXES = ("y_lo", "z_pair", "z_bit", "core", "y_hi", "x")
SEQ = ("y_lo", "z_pair", "z_bit", "core")
Z = ("z_pair", "z_bit")
HEAD = ("y_hi", "x")
F32 = jnp.float32
BF16 = jnp.bfloat16


def iota(shape, axis):
    return lax.broadcasted_iota(jnp.int32, shape, axis)


def ones_where(mask):
    return jnp.where(mask, 1.0, 0.0).astype(BF16)


def mm(a, b):
    return jnp.dot(a, b, preferred_element_type=F32)


def mm_t(a, b):
    return lax.dot_general(a, b, (((1,), (1,)), ((), ())), preferred_element_type=F32)


def t_mm(a, b):
    return lax.dot_general(a, b, (((0,), (0,)), ((), ())), preferred_element_type=F32)


def split(value, parts):
    pieces = []
    for _ in range(parts):
        piece = value.astype(BF16)
        pieces.append(piece)
        value = value - piece.astype(F32)
    return pieces


def silu(value):
    return value * (1.0 / (1.0 + jnp.exp(-value)))


def reversal(size):
    return ones_where(iota((size, size), 0) + iota((size, size), 1) == size - 1)


def spread(value, width):
    table = ones_where(iota((128, width), 0) == iota((128, width), 1) // HEAD_DIM)
    return sum(mm(piece, table) for piece in split(value, 2))


def running_sum(rate):
    lower = ones_where(iota((SPAN, SPAN), 0) >= iota((SPAN, SPAN), 1))
    return sum(mm(lower, piece) for piece in split(rate, 3))


def assemble(place_ref, pieces, full_ref):
    bit, core = place_ref[1], place_ref[2]
    for side in range(2):
        near, left, right = pieces[3 * side : 3 * side + 3]
        column = core + side - 2 * core * side
        for block in range(16):
            far = left.at[block] if block < 8 else right.at[block - 8]
            start = 128 * block + 32 * column
            full_ref[pl.ds(pl.multiple_of(start + 64 * bit, 32), 32)] = near[block]
            full_ref[pl.ds(pl.multiple_of(start + 64 * (1 - bit), 32), 32)] = far[...]


def assemble_ring(place_ref, pieces, full_ref):
    core, y_lo = place_ref[2], place_ref[3]
    for side in range(2):
        column = core + side - 2 * core * side
        for step in range(4):
            y = (y_lo + 4 - step) % 4
            for z in range(8):
                start = 512 * y + 64 * z + 32 * column
                full_ref[pl.ds(pl.multiple_of(start, 32), 32)] = pieces[side][z, step]


def front_kernel(
    place_ref, x_ref, n0, l0, r0, n1, l1, r1, bias_ref, decay_ref, taps_ref,
    send_ref, stream_ref, conv_ref, step_ref, rows_ref, full_ref,
):
    assemble(place_ref, (n0, l0, r0, n1, l1, r1), full_ref)
    flip_rows, flip_columns = reversal(EXT), reversal(256)
    for block in range(8):
        columns = slice(block * 256, (block + 1) * 256)
        stream_ref[:EXT, columns] = x_ref[block, :EXT]
        turned = mm(x_ref[7 - block, HALO:], flip_columns).astype(BF16)
        stream_ref[EXT:, columns] = mm(flip_rows, turned).astype(BF16)
    proj = mm(stream_ref[...], full_ref[...])
    conv_width = conv_ref.shape[2]
    rows_ref[...] = proj[:, :conv_width].astype(BF16).astype(F32)
    for branch in range(2):
        base = branch * EXT + HALO - (CONV - 1)
        running = taps_ref[0:1] * rows_ref[base : base + SPAN]
        for tap in range(1, CONV):
            running = running + taps_ref[tap : tap + 1] * rows_ref[base + tap : base + tap + SPAN]
        convolved = silu(running).astype(BF16)
        conv_ref[branch] = convolved
        raw = proj[branch * EXT + HALO : (branch + 1) * EXT, conv_width:] + bias_ref[...]
        step = jnp.maximum(raw, 0.0) + jnp.log1p(jnp.exp(-jnp.abs(raw)))
        cum = running_sum(step * -jnp.exp(decay_ref[...]))
        step_ref[branch] = step
        end = cum[SPAN - 1 : SPAN]
        x_width = conv_width - STATE
        weighted = (
            convolved[:, :x_width].astype(F32) * spread(jnp.exp(end - cum) * step, x_width)
        ).astype(BF16)
        state = t_mm(weighted, convolved[:, x_width:])
        high, low = (piece.astype(F32) for piece in split(jnp.exp(end), 2))
        row = iota((8, 128), 0)
        tiles = []
        for head in range(x_width // HEAD_DIM):
            tile = jnp.where(row == 0, high[:, head : head + 1], jnp.where(row == 1, low[:, head : head + 1], 0.0))
            tiles += [tile[None]] * 4
        count = x_width // 16
        send_ref[branch * count : (branch + 1) * count] = jnp.concatenate(
            [state.reshape(count, 16, STATE), jnp.concatenate(tiles, 0)], 1
        ).astype(BF16)


def scan_kernel(place_ref, got_ref, entry_ref):
    blocks = got_ref.shape[0]
    backward = jnp.where(place_ref[0] >= blocks // 2, 1, 0)

    def one(lap, state):
        block = lap + backward * (blocks - 1 - 2 * lap)
        entry_ref[block] = state.astype(BF16)
        got = got_ref[block].astype(F32)
        return state * (got[16:17] + got[17:18]) + got[:16]

    lax.fori_loop(0, blocks, one, jnp.zeros((16, STATE), F32), unroll=4)


def back_kernel(
    place_ref, stream_ref, own_ref, other_ref, conv_ref, step_ref, entry_ref, decay_ref, taps_ref, skip_ref, gain_ref,
    out_ref, rows_ref, inner_ref, full_ref,
):
    assemble_ring(place_ref, (own_ref, other_ref), full_ref)
    width = inner_ref.shape[1]
    proj = mm(stream_ref[...], full_ref[:, width:])
    rows_ref[...] = proj[:, width:].astype(BF16).astype(F32)
    causal = iota((SPAN, SPAN), 0) >= iota((SPAN, SPAN), 1)
    normed = []
    for branch in range(2):
        gate = silu(proj[branch * EXT + HALO : (branch + 1) * EXT, :width].astype(BF16).astype(F32))
        base = branch * EXT + HALO - (CONV - 1)
        running = taps_ref[0:1] * rows_ref[base : base + SPAN]
        for tap in range(1, CONV):
            running = running + taps_ref[tap : tap + 1] * rows_ref[base + tap : base + tap + SPAN]
        out_map = silu(running).astype(BF16)
        scores = mm_t(out_map, conv_ref[branch, :, width:])
        step = step_ref[branch]
        cum = running_sum(step * -jnp.exp(decay_ref[...]))
        cum_t, step_t = cum.T, step.T
        for head in range(width // HEAD_DIM):
            channels = slice(head * HEAD_DIM, (head + 1) * HEAD_DIM)
            differ = cum[:, head : head + 1] - cum_t[head : head + 1]
            decay = jnp.where(causal, jnp.exp(jnp.where(causal, differ, 0.0)), 0.0)
            weights = (scores * decay * step_t[head : head + 1]).astype(BF16)
            x_head = conv_ref[branch, :, channels]
            inner_ref[:, channels] = mm(weights, x_head) + skip_ref[:, channels] * x_head.astype(F32)
        entry = entry_ref[branch * width : (branch + 1) * width]
        carried = mm_t(out_map, entry) * spread(jnp.exp(cum), width)
        gated = (inner_ref[...] + carried) * gate
        square = jnp.mean(gated * gated, axis=-1, keepdims=True)
        normed.append((gated * lax.rsqrt(square + 1e-05) * gain_ref[...]).astype(BF16))
    forward, mirror = normed[0], mm(reversal(SPAN), normed[1]).astype(BF16)
    flip = reversal(256)
    for block in range(8):
        near, far = (slice(part * 256, (part + 1) * 256) for part in (block, 7 - block))
        turned = mm(flip, full_ref[far, :width]).astype(BF16)
        out_ref[block] = (mm_t(forward, full_ref[near, :width]) + mm_t(mirror, turned)).astype(BF16)


def kernel_call(body, outs, scratch, in_specs=None):
    extra = {} if in_specs is None else {"in_specs": in_specs}
    return pl.pallas_call(
        body,
        out_shape=outs,
        scratch_shapes=scratch,
        compiler_params=pltpu.CompilerParams(vmem_limit_bytes=20 << 20),
        **extra,
    )


def copies(block, axis):
    count = lax.axis_size(axis)
    return lax.all_to_all(jnp.broadcast_to(block[None], (count, *block.shape)), axis, 0, 0, tiled=True)


def shifted(value, steps):
    count = lax.axis_size(SEQ)
    route = [(source, source + steps) for source in range(count) if 0 <= source + steps < count]
    return lax.ppermute(value, SEQ, route)


def swapped(block):
    return lax.ppermute(block, "core", [(0, 1), (1, 0)])


def neighbours(near):
    count, half = lax.axis_size(Z), near.shape[0] // 2
    left = lax.ppermute(near[:half], Z, [(z, (z + 1) % count) for z in range(count)])
    right = lax.ppermute(near[half:], Z, [(z, (z - 1) % count) for z in range(count)])
    return left, right


def around(block, axis):
    count = lax.axis_size(axis)
    steps = [
        lax.ppermute(block, axis, [(place, (place + step) % count) for place in range(count)])
        for step in range(1, count)
    ]
    return jnp.stack([block, *steps])


def together(*values):
    return lax.optimization_barrier(values)


def local(
    layer_input, w_input, w_gate, w_maps, w_step, step_bias, decay_log, skip_gain, conv_input, conv_maps, norm_gain, w_out,
):
    rows, features = layer_input.shape
    width, heads = w_input.shape[1], w_step.shape[1]
    wide = 128 - heads
    place = jnp.stack([lax.axis_index(SEQ), lax.axis_index("z_bit"), lax.axis_index("core"), lax.axis_index("y_lo")])
    first = jnp.concatenate(
        [w_input, w_maps[:, :STATE], w_step, jnp.zeros((w_step.shape[0], wide), BF16)], 1
    )
    second = jnp.concatenate([w_out.T, w_gate, w_maps[:, STATE:]], 1)
    near = copies(first, ("y_lo", "z_pair"))
    before = shifted(layer_input[rows - HALO :], 1)
    after = shifted(layer_input[:HALO], -1)
    second_y = around(second, "y_lo")
    near, second_y, extended = together(near, second_y, jnp.concatenate([before, layer_input, after]))
    second_z = lax.all_gather(second_y, Z)
    left, right = neighbours(near)
    blocks = copies(extended, HEAD)
    first_pieces = (near, left, right, swapped(near), swapped(left), swapped(right))
    smem = pl.BlockSpec(memory_space=pltpu.SMEM)
    vmem = pl.BlockSpec(memory_space=pltpu.VMEM)
    struct = jax.ShapeDtypeStruct
    places = 2 * width // 16
    send, stream, conv, step = kernel_call(
        front_kernel,
        (
            struct((places, 24, STATE), BF16),
            struct((2 * EXT, 8 * features), BF16),
            struct((2, SPAN, width + STATE), BF16),
            struct((2, SPAN, 128), F32),
        ),
        [pltpu.VMEM((2 * EXT, width + STATE), F32), pltpu.VMEM((8 * features, width + 2 * STATE), BF16)],
        [smem] + [vmem] * 10,
    )(
        place, blocks, *first_pieces,
        jnp.pad(step_bias, (0, wide))[None], jnp.pad(decay_log, (0, wide))[None],
        jnp.concatenate([conv_input, conv_maps[:, :STATE]], 1),
    )
    got = lax.all_to_all(send, SEQ, 0, 0, tiled=True)
    second_own, got = together(second_z, got)
    second_other = swapped(second_own)
    entries = kernel_call(scan_kernel, struct((places, 16, STATE), BF16), [], [smem, vmem])(place, got)
    entry = lax.all_to_all(entries, SEQ, 0, 0, tiled=True).reshape(2 * width, STATE)
    partial = kernel_call(
        back_kernel,
        struct((8, SPAN, features), BF16),
        [
            pltpu.VMEM((2 * EXT, STATE), F32),
            pltpu.VMEM((SPAN, width), F32),
            pltpu.VMEM((8 * features, 2 * width + STATE), BF16),
        ],
        [smem] + [vmem] * 10,
    )(
        place, stream, second_own, second_other, conv, step, entry, jnp.pad(decay_log, (0, wide))[None], conv_maps[:, STATE:],
        jnp.repeat(skip_gain, HEAD_DIM)[None], norm_gain[None],
    )
    parts = lax.all_to_all(partial, HEAD, 0, 0, tiled=True)
    return jnp.sum(parts.astype(F32), 0).astype(BF16)


def solution(mesh):
    fine = Mesh(mesh.devices.reshape(4, 4, 2, 2, 2, 4), AXES)
    placed = (
        P(SEQ, HEAD), P(SEQ, HEAD), P(SEQ, HEAD), P(SEQ, None), P(SEQ, HEAD), P(HEAD), P(HEAD), P(HEAD), P(None, HEAD), P(), P(HEAD), P(HEAD, SEQ),
    )
    return jax.shard_map(local, mesh=fine, in_specs=placed, out_specs=P(SEQ, HEAD), check_vma=False)
```

```python
import jax
import jax.numpy as jnp
from jax import lax
from jax.experimental import pallas as pl
from jax.experimental.pallas import tpu as pltpu
from jax.sharding import Mesh
from jax.sharding import PartitionSpec as P

HEAD_DIM = 64
SPAN = 128
CONV = 4
STATE = 128
HALO = 16
EXT = SPAN + HALO
AXES = ("y_lo", "z_pair", "z_bit", "core", "y_hi", "x")
SEQ = ("y_lo", "z_pair", "z_bit", "core")
Z = ("z_pair", "z_bit")
HEAD = ("y_hi", "x")
F32 = jnp.float32
BF16 = jnp.bfloat16


def iota(shape, axis):
    return lax.broadcasted_iota(jnp.int32, shape, axis)


def ones_where(mask):
    return jnp.where(mask, 1.0, 0.0).astype(BF16)


def mm(a, b):
    return jnp.dot(a, b, preferred_element_type=F32)


def mm_t(a, b):
    return lax.dot_general(a, b, (((1,), (1,)), ((), ())), preferred_element_type=F32)


def t_mm(a, b):
    return lax.dot_general(a, b, (((0,), (0,)), ((), ())), preferred_element_type=F32)


def split(value, parts):
    pieces = []
    for _ in range(parts):
        piece = value.astype(BF16)
        pieces.append(piece)
        value = value - piece.astype(F32)
    return pieces


def silu(value):
    return value * (1.0 / (1.0 + jnp.exp(-value)))


def reversal(size):
    return ones_where(iota((size, size), 0) + iota((size, size), 1) == size - 1)


def spread(value, width):
    table = ones_where(iota((128, width), 0) == iota((128, width), 1) // HEAD_DIM)
    return sum(mm(piece, table) for piece in split(value, 2))


def running_sum(rate):
    lower = ones_where(iota((SPAN, SPAN), 0) >= iota((SPAN, SPAN), 1))
    return sum(mm(lower, piece) for piece in split(rate, 3))


def assemble(place_ref, pieces, full_ref):
    bit, core = place_ref[1], place_ref[2]
    for side in range(2):
        near, left, right = pieces[3 * side : 3 * side + 3]
        column = core + side - 2 * core * side
        for block in range(16):
            far = left.at[block] if block < 8 else right.at[block - 8]
            start = 128 * block + 32 * column
            full_ref[pl.ds(pl.multiple_of(start + 64 * bit, 32), 32)] = near[block]
            full_ref[pl.ds(pl.multiple_of(start + 64 * (1 - bit), 32), 32)] = far[...]


def assemble_ring(place_ref, pieces, full_ref):
    core, y_lo = place_ref[2], place_ref[3]
    for side in range(2):
        column = core + side - 2 * core * side
        for step in range(4):
            y = (y_lo + 4 - step) % 4
            for z in range(8):
                start = 512 * y + 64 * z + 32 * column
                full_ref[pl.ds(pl.multiple_of(start, 32), 32)] = pieces[side][z, step]


def front_kernel(
    place_ref, x_ref, n0, l0, r0, n1, l1, r1, small_ref,
    send_ref, stream_ref, conv_ref, step_ref, rows_ref, full_ref,
):
    assemble(place_ref, (n0, l0, r0, n1, l1, r1), full_ref)
    y_hi, x = place_ref[4], place_ref[5]
    flip_rows, flip_columns = reversal(EXT), reversal(256)
    for step in range(4):
        for side in range(2):
            block = 4 * (y_hi + side - 2 * y_hi * side) + (x + 4 - step) % 4
            stream_ref[:EXT, pl.ds(pl.multiple_of(block * 256, 256), 256)] = x_ref[step, side, :EXT]
            turned = mm(x_ref[step, side, HALO:], flip_columns).astype(BF16)
            stream_ref[EXT:, pl.ds(pl.multiple_of((7 - block) * 256, 256), 256)] = mm(flip_rows, turned).astype(BF16)
    proj = mm(stream_ref[...], full_ref[...])
    conv_width = conv_ref.shape[2]
    taps, bias, decay = small_ref[:CONV], small_ref[4:5, :128], small_ref[5:6, :128]
    rows_ref[...] = proj[:, :conv_width].astype(BF16).astype(F32)
    for branch in range(2):
        base = branch * EXT + HALO - (CONV - 1)
        running = taps[0:1] * rows_ref[base : base + SPAN]
        for tap in range(1, CONV):
            running = running + taps[tap : tap + 1] * rows_ref[base + tap : base + tap + SPAN]
        convolved = silu(running).astype(BF16)
        conv_ref[branch] = convolved
        raw = proj[branch * EXT + HALO : (branch + 1) * EXT, conv_width:] + bias
        step = jnp.maximum(raw, 0.0) + jnp.log1p(jnp.exp(-jnp.abs(raw)))
        cum = running_sum(step * -jnp.exp(decay))
        step_ref[branch] = step
        end = cum[SPAN - 1 : SPAN]
        x_width = conv_width - STATE
        weighted = (
            convolved[:, :x_width].astype(F32) * spread(jnp.exp(end - cum) * step, x_width)
        ).astype(BF16)
        state = t_mm(weighted, convolved[:, x_width:])
        high, low = (piece.astype(F32) for piece in split(jnp.exp(end), 2))
        row = iota((8, 128), 0)
        tiles = []
        for head in range(x_width // HEAD_DIM):
            tile = jnp.where(row == 0, high[:, head : head + 1], jnp.where(row == 1, low[:, head : head + 1], 0.0))
            tiles += [tile[None]] * 4
        count = x_width // 16
        send_ref[branch * count : (branch + 1) * count] = jnp.concatenate(
            [state.reshape(count, 16, STATE), jnp.concatenate(tiles, 0)], 1
        ).astype(BF16)


def scan_kernel(place_ref, got_ref, entry_ref):
    blocks = got_ref.shape[0]
    backward = jnp.where(place_ref[0] >= blocks // 2, 1, 0)

    def one(lap, state):
        block = lap + backward * (blocks - 1 - 2 * lap)
        entry_ref[block] = state.astype(BF16)
        got = got_ref[block].astype(F32)
        return state * (got[16:17] + got[17:18]) + got[:16]

    lax.fori_loop(0, blocks, one, jnp.zeros((16, STATE), F32), unroll=4)


def back_kernel(
    place_ref, stream_ref, own_ref, other_ref, conv_ref, step_ref, entry_ref, small_ref,
    out_ref, rows_ref, inner_ref, full_ref,
):
    assemble_ring(place_ref, (own_ref, other_ref), full_ref)
    width = inner_ref.shape[1]
    proj = mm(stream_ref[...], full_ref[:, width:])
    taps, log_rate = small_ref[:CONV, :STATE], small_ref[6:7, :128]
    rows_ref[...] = proj[:, width:].astype(BF16).astype(F32)
    causal = iota((SPAN, SPAN), 0) >= iota((SPAN, SPAN), 1)
    normed = []
    for branch in range(2):
        gate = silu(proj[branch * EXT + HALO : (branch + 1) * EXT, :width].astype(BF16).astype(F32))
        base = branch * EXT + HALO - (CONV - 1)
        running = taps[0:1] * rows_ref[base : base + SPAN]
        for tap in range(1, CONV):
            running = running + taps[tap : tap + 1] * rows_ref[base + tap : base + tap + SPAN]
        out_map = silu(running).astype(BF16)
        scores = mm_t(out_map, conv_ref[branch, :, width:])
        step = step_ref[branch]
        cum = running_sum(step * -jnp.exp(log_rate))
        cum_t, step_t = cum.T, step.T
        for head in range(width // HEAD_DIM):
            channels = slice(head * HEAD_DIM, (head + 1) * HEAD_DIM)
            differ = cum[:, head : head + 1] - cum_t[head : head + 1]
            decay = jnp.where(causal, jnp.exp(jnp.where(causal, differ, 0.0)), 0.0)
            weights = (scores * decay * step_t[head : head + 1]).astype(BF16)
            x_head = conv_ref[branch, :, channels]
            inner_ref[:, channels] = mm(weights, x_head) + small_ref[4:5, channels] * x_head.astype(F32)
        entry = entry_ref[branch * width : (branch + 1) * width]
        carried = mm_t(out_map, entry) * spread(jnp.exp(cum), width)
        gated = (inner_ref[...] + carried) * gate
        square = jnp.mean(gated * gated, axis=-1, keepdims=True)
        normed.append((gated * lax.rsqrt(square + 1e-05) * small_ref[5:6]).astype(BF16))
    forward, mirror = normed[0], mm(reversal(SPAN), normed[1]).astype(BF16)
    flip = reversal(256)
    for block in range(8):
        near, far = (slice(part * 256, (part + 1) * 256) for part in (block, 7 - block))
        turned = mm(flip, full_ref[far, :width]).astype(BF16)
        out_ref[block % 4, block // 4] = (mm_t(forward, full_ref[near, :width]) + mm_t(mirror, turned)).astype(BF16)


def kernel_call(body, outs, scratch, in_specs=None):
    extra = {} if in_specs is None else {"in_specs": in_specs}
    return pl.pallas_call(
        body,
        out_shape=outs,
        scratch_shapes=scratch,
        compiler_params=pltpu.CompilerParams(vmem_limit_bytes=18 << 20),
        **extra,
    )


def copies(block, axis):
    count = lax.axis_size(axis)
    return lax.all_to_all(jnp.broadcast_to(block[None], (count, *block.shape)), axis, 0, 0, tiled=True)


def shifted(value, steps):
    count = lax.axis_size(SEQ)
    route = [(source, source + steps) for source in range(count) if 0 <= source + steps < count]
    return lax.ppermute(value, SEQ, route)


def swapped(block):
    return lax.ppermute(block, "core", [(0, 1), (1, 0)])


def neighbours(near):
    count, half = lax.axis_size(Z), near.shape[0] // 2
    left = lax.ppermute(near[:half], Z, [(z, (z + 1) % count) for z in range(count)])
    right = lax.ppermute(near[half:], Z, [(z, (z - 1) % count) for z in range(count)])
    return left, right


def around(block, axis):
    count = lax.axis_size(axis)
    steps = [
        lax.ppermute(block, axis, [(place, (place + step) % count) for place in range(count)])
        for step in range(1, count)
    ]
    return jnp.stack([block, *steps])


def together(*values):
    return lax.optimization_barrier(values)


def local(
    layer_input, w_input, w_gate, w_maps, w_step, step_bias, decay_log, skip_gain, conv_input, conv_maps, norm_gain, w_out,
):
    rows, features = layer_input.shape
    width, heads = w_input.shape[1], w_step.shape[1]
    wide = 128 - heads
    place = jnp.stack([lax.axis_index(SEQ), lax.axis_index("z_bit"), lax.axis_index("core")] + [lax.axis_index(axis) for axis in ("y_lo", "y_hi", "x")])
    first = jnp.concatenate(
        [w_input, w_maps[:, :STATE], w_step, jnp.zeros((w_step.shape[0], wide), BF16)], 1
    )
    second = jnp.concatenate([w_out.T, w_gate, w_maps[:, STATE:]], 1)
    near = copies(first, ("y_lo", "z_pair"))
    before = shifted(layer_input[rows - HALO :], 1)
    after = shifted(layer_input[:HALO], -1)
    extended = jnp.concatenate([before, layer_input, after])
    extended = jnp.stack([extended, lax.ppermute(extended, "y_hi", [(0, 1), (1, 0)])])
    second_y = around(second, "y_lo")
    near, second_y, extended = together(near, second_y, extended)
    second_z = lax.all_gather(second_y, Z)
    left, right = neighbours(near)
    blocks = around(extended, "x")
    first_pieces = (near, left, right, swapped(near), swapped(left), swapped(right))
    smem = pl.BlockSpec(memory_space=pltpu.SMEM)
    vmem = pl.BlockSpec(memory_space=pltpu.VMEM)
    struct = jax.ShapeDtypeStruct
    places = 2 * width // 16
    front_small = jnp.concatenate(
        [jnp.concatenate([conv_input, conv_maps[:, :STATE]], 1)]
        + [jnp.pad(value, (0, width + STATE - heads))[None] for value in (step_bias, decay_log)]
    )
    back_small = jnp.concatenate(
        [
            jnp.pad(conv_maps[:, STATE:], ((0, 0), (0, width - STATE))),
            jnp.repeat(skip_gain, HEAD_DIM)[None],
            norm_gain[None],
            jnp.pad(decay_log, (0, width - heads))[None],
        ]
    )
    send, stream, conv, step = kernel_call(
        front_kernel,
        (
            struct((places, 24, STATE), BF16),
            struct((2 * EXT, 8 * features), BF16),
            struct((2, SPAN, width + STATE), BF16),
            struct((2, SPAN, 128), F32),
        ),
        [pltpu.VMEM((2 * EXT, width + STATE), F32), pltpu.VMEM((8 * features, width + 2 * STATE), BF16)],
        [smem] + [vmem] * 8,
    )(
        place, blocks, *first_pieces, front_small,
    )
    got = lax.all_to_all(send, SEQ, 0, 0, tiled=True)
    second_own, got = together(second_z, got)
    second_other = swapped(second_own)
    entries = kernel_call(scan_kernel, struct((places, 16, STATE), BF16), [], [smem, vmem])(place, got)
    entry = lax.all_to_all(entries, SEQ, 0, 0, tiled=True).reshape(2 * width, STATE)
    partial = kernel_call(
        back_kernel,
        struct((4, 2, SPAN, features), BF16),
        [
            pltpu.VMEM((2 * EXT, STATE), F32),
            pltpu.VMEM((SPAN, width), F32),
            pltpu.VMEM((8 * features, 2 * width + STATE), BF16),
        ],
        [smem] + [vmem] * 7,
    )(
        place, stream, second_own, second_other, conv, step, entry, back_small,
    )
    parts = jnp.sum(lax.all_to_all(partial, "x", 0, 0, tiled=True).astype(F32), 0)
    low = lax.axis_index("y_hi") == 0
    kept, sent = jnp.where(low, parts[0], parts[1]), jnp.where(low, parts[1], parts[0]).astype(BF16)
    return (kept + lax.ppermute(sent, "y_hi", [(0, 1), (1, 0)]).astype(F32)).astype(BF16)


def solution(mesh):
    fine = Mesh(mesh.devices.reshape(4, 4, 2, 2, 2, 4), AXES)
    placed = (
        P(SEQ, HEAD), P(SEQ, HEAD), P(SEQ, HEAD), P(SEQ, None), P(SEQ, HEAD), P(HEAD), P(HEAD), P(HEAD), P(None, HEAD), P(), P(HEAD), P(HEAD, SEQ),
    )
    return jax.shard_map(local, mesh=fine, in_specs=placed, out_specs=P(SEQ, HEAD), check_vma=False)
```

```python
import jax
import jax.numpy as jnp
from jax import lax
from jax.experimental import pallas as pl
from jax.experimental.pallas import tpu as pltpu
from jax.sharding import Mesh
from jax.sharding import PartitionSpec as P

HEAD_DIM = 64
SPAN = 128
CONV = 4
STATE = 128
HALO = 16
EXT = SPAN + HALO
AXES = ("y_lo", "z_pair", "z_bit", "core", "y_hi", "x")
SEQ = ("y_lo", "z_pair", "z_bit", "core")
Z = ("z_pair", "z_bit")
HEAD = ("y_hi", "x")
F32 = jnp.float32
BF16 = jnp.bfloat16


def iota(shape, axis):
    return lax.broadcasted_iota(jnp.int32, shape, axis)


def ones_where(mask):
    return jnp.where(mask, 1.0, 0.0).astype(BF16)


def mm(a, b):
    return jnp.dot(a, b, preferred_element_type=F32)


def mm_t(a, b):
    return lax.dot_general(a, b, (((1,), (1,)), ((), ())), preferred_element_type=F32)


def t_mm(a, b):
    return lax.dot_general(a, b, (((0,), (0,)), ((), ())), preferred_element_type=F32)


def split(value, parts):
    pieces = []
    for _ in range(parts):
        piece = value.astype(BF16)
        pieces.append(piece)
        value = value - piece.astype(F32)
    return pieces


def silu(value):
    return value * (1.0 / (1.0 + jnp.exp(-value)))


def reversal(size):
    return ones_where(iota((size, size), 0) + iota((size, size), 1) == size - 1)


def spread(value, width):
    table = ones_where(iota((128, width), 0) == iota((128, width), 1) // HEAD_DIM)
    return sum(mm(piece, table) for piece in split(value, 2))


def running_sum(rate):
    lower = ones_where(iota((SPAN, SPAN), 0) >= iota((SPAN, SPAN), 1))
    return sum(mm(lower, piece) for piece in split(rate, 3))


def assemble(place_ref, pieces, full_ref):
    bit, core = place_ref[1], place_ref[2]
    for side in range(2):
        near, left, right = pieces[3 * side : 3 * side + 3]
        column = core + side - 2 * core * side
        for block in range(16):
            far = left.at[block] if block < 8 else right.at[block - 8]
            start = 128 * block + 32 * column
            full_ref[pl.ds(pl.multiple_of(start + 64 * bit, 32), 32)] = near[block]
            full_ref[pl.ds(pl.multiple_of(start + 64 * (1 - bit), 32), 32)] = far[...]


def pack_kernel(input_ref, maps_ref, step_ref, out_ref):
    heads = step_ref.shape[0]
    step = t_mm(step_ref[...], ones_where(iota((heads, 128), 0) == iota((heads, 128), 1))).astype(BF16)
    block = jnp.concatenate([input_ref[...], maps_ref[:, :STATE], step], 1)
    for copy in range(out_ref.shape[0]):
        out_ref[copy] = block


def front_kernel(
    place_ref, x_ref, n0, l0, r0, n1, l1, r1, small_ref,
    send_ref, stream_ref, conv_ref, step_ref, rows_ref, full_ref,
):
    assemble(place_ref, (n0, l0, r0, n1, l1, r1), full_ref)
    y_hi = place_ref[4]
    flip_rows, flip_columns = reversal(EXT), reversal(256)
    for step in range(4):
        for side in range(2):
            block = 4 * (y_hi + side - 2 * y_hi * side) + step
            stream_ref[:EXT, pl.ds(pl.multiple_of(block * 256, 256), 256)] = x_ref[step, side, :EXT]
            turned = mm(x_ref[step, side, HALO:], flip_columns).astype(BF16)
            stream_ref[EXT:, pl.ds(pl.multiple_of((7 - block) * 256, 256), 256)] = mm(flip_rows, turned).astype(BF16)
    proj = mm(stream_ref[...], full_ref[...])
    conv_width = conv_ref.shape[2]
    taps, bias, decay = small_ref[:CONV], small_ref[4:5, :128], small_ref[5:6, :128]
    rows_ref[...] = proj[:, :conv_width].astype(BF16).astype(F32)
    for branch in range(2):
        base = branch * EXT + HALO - (CONV - 1)
        running = taps[0:1] * rows_ref[base : base + SPAN]
        for tap in range(1, CONV):
            running = running + taps[tap : tap + 1] * rows_ref[base + tap : base + tap + SPAN]
        convolved = silu(running).astype(BF16)
        conv_ref[branch] = convolved
        raw = proj[branch * EXT + HALO : (branch + 1) * EXT, conv_width:] + bias
        step = jnp.maximum(raw, 0.0) + jnp.log1p(jnp.exp(-jnp.abs(raw)))
        cum = running_sum(step * -jnp.exp(decay))
        step_ref[branch] = step
        end = cum[SPAN - 1 : SPAN]
        x_width = conv_width - STATE
        weighted = (
            convolved[:, :x_width].astype(F32) * spread(jnp.exp(end - cum) * step, x_width)
        ).astype(BF16)
        state = t_mm(weighted, convolved[:, x_width:])
        high, low = (piece.astype(F32) for piece in split(jnp.exp(end), 2))
        row = iota((8, 128), 0)
        tiles = []
        for head in range(x_width // HEAD_DIM):
            tile = jnp.where(row == 0, high[:, head : head + 1], jnp.where(row == 1, low[:, head : head + 1], 0.0))
            tiles += [tile[None]] * 4
        count = x_width // 16
        send_ref[branch * count : (branch + 1) * count] = jnp.concatenate(
            [state.reshape(count, 16, STATE), jnp.concatenate(tiles, 0)], 1
        ).astype(BF16)


def scan_kernel(place_ref, got_ref, entry_ref):
    blocks = got_ref.shape[0]
    backward = jnp.where(place_ref[0] >= blocks // 2, 1, 0)

    def one(lap, state):
        block = lap + backward * (blocks - 1 - 2 * lap)
        entry_ref[block] = state.astype(BF16)
        got = got_ref[block].astype(F32)
        return state * (got[16:17] + got[17:18]) + got[:16]

    lax.fori_loop(0, blocks, one, jnp.zeros((16, STATE), F32), unroll=4)


def inner_kernel(
    place_ref, stream_ref, own_ref, other_ref, conv_ref, step_ref, small_ref,
    map_ref, inner_ref, gate_ref, weights_ref, rows_ref, full_ref,
):
    core, y_lo = place_ref[2], place_ref[3]
    width = inner_ref.shape[2]
    for side, ref in enumerate((own_ref, other_ref)):
        column = core + side - 2 * core * side
        for step in range(4):
            y = (y_lo + 4 - step) % 4
            for z in range(8):
                start = pl.ds(pl.multiple_of(512 * y + 64 * z + 32 * column, 32), 32)
                weights_ref[0, start] = ref[z, step, :, :width]
                full_ref[start] = ref[z, step, :, width:]
    proj = mm(stream_ref[...], full_ref[...])
    taps, log_rate = small_ref[:CONV, :STATE], small_ref[6:7, :128]
    rows_ref[...] = proj[:, width:].astype(BF16).astype(F32)
    causal = iota((SPAN, SPAN), 0) >= iota((SPAN, SPAN), 1)
    for branch in range(2):
        gate = silu(proj[branch * EXT + HALO : (branch + 1) * EXT, :width].astype(BF16).astype(F32))
        base = branch * EXT + HALO - (CONV - 1)
        running = taps[0:1] * rows_ref[base : base + SPAN]
        for tap in range(1, CONV):
            running = running + taps[tap : tap + 1] * rows_ref[base + tap : base + tap + SPAN]
        out_map = silu(running).astype(BF16)
        map_ref[branch] = out_map
        scores = mm_t(out_map, conv_ref[branch, :, width:])
        step = step_ref[branch]
        cum = running_sum(step * -jnp.exp(log_rate))
        cum_t, step_t = cum.T, step.T
        for head in range(width // HEAD_DIM):
            channels = slice(head * HEAD_DIM, (head + 1) * HEAD_DIM)
            differ = cum[:, head : head + 1] - cum_t[head : head + 1]
            decay = jnp.where(causal, jnp.exp(jnp.where(causal, differ, 0.0)), 0.0)
            weights = (scores * decay * step_t[head : head + 1]).astype(BF16)
            x_head = conv_ref[branch, :, channels]
            inner_ref[branch, :, channels] = mm(weights, x_head) + small_ref[4:5, channels] * x_head.astype(F32)
        inner_ref[branch] = inner_ref[branch] * gate
        gate_ref[branch] = spread(jnp.exp(cum), width) * gate
    flip = reversal(256)
    for block in range(8):
        near, far = (slice(part * 256, (part + 1) * 256) for part in (block, 7 - block))
        weights_ref[1, near] = mm(flip, weights_ref[0, far]).astype(BF16)


def out_kernel(entry_ref, map_ref, inner_ref, gate_ref, weights_ref, small_ref, out_ref):
    width = inner_ref.shape[2]
    normed = []
    for branch in range(2):
        carried = mm_t(map_ref[branch], entry_ref[branch * width : (branch + 1) * width])
        gated = inner_ref[branch] + carried * gate_ref[branch]
        square = jnp.mean(gated * gated, axis=-1, keepdims=True)
        normed.append((gated * lax.rsqrt(square + 1e-05) * small_ref[5:6]).astype(BF16))
    forward, mirror = normed[0], mm(reversal(SPAN), normed[1]).astype(BF16)
    for block in range(8):
        rows = slice(block * 256, (block + 1) * 256)
        out_ref[block % 4, block // 4] = (
            mm_t(forward, weights_ref[0, rows]) + mm_t(mirror, weights_ref[1, rows])
        ).astype(BF16)


def kernel_call(body, outs, scratch, in_specs=None):
    extra = {} if in_specs is None else {"in_specs": in_specs}
    return pl.pallas_call(
        body,
        out_shape=outs,
        scratch_shapes=scratch,
        compiler_params=pltpu.CompilerParams(vmem_limit_bytes=20 << 20),
        **extra,
    )


def copies(block, axis):
    count = lax.axis_size(axis)
    return lax.all_to_all(jnp.broadcast_to(block[None], (count, *block.shape)), axis, 0, 0, tiled=True)


def shifted(value, steps):
    count = lax.axis_size(SEQ)
    route = [(source, source + steps) for source in range(count) if 0 <= source + steps < count]
    return lax.ppermute(value, SEQ, route)


def swapped(block):
    return lax.ppermute(block, "core", [(0, 1), (1, 0)])


def neighbours(near):
    count, half = lax.axis_size(Z), near.shape[0] // 2
    left = lax.ppermute(near[:half], Z, [(z, (z + 1) % count) for z in range(count)])
    right = lax.ppermute(near[half:], Z, [(z, (z - 1) % count) for z in range(count)])
    return left, right


def around(block, axis):
    count = lax.axis_size(axis)
    steps = [
        lax.ppermute(block, axis, [(place, (place + step) % count) for place in range(count)])
        for step in range(1, count)
    ]
    return jnp.stack([block, *steps])


def together(*values):
    return lax.optimization_barrier(values)


def local(
    layer_input, w_input, w_gate, w_maps, w_step, step_bias, decay_log, skip_gain, conv_input, conv_maps, norm_gain, w_out,
):
    rows, features = layer_input.shape
    width, heads = w_input.shape[1], w_step.shape[1]
    wide = 128 - heads
    place = jnp.stack([lax.axis_index(SEQ), lax.axis_index("z_bit"), lax.axis_index("core")] + [lax.axis_index(axis) for axis in ("y_lo", "y_hi")])
    smem = pl.BlockSpec(memory_space=pltpu.SMEM)
    vmem = pl.BlockSpec(memory_space=pltpu.VMEM)
    struct = jax.ShapeDtypeStruct
    first = kernel_call(pack_kernel, struct((16, w_input.shape[0], width + 2 * STATE), BF16), [])(
        w_input, w_maps, w_step.T
    )
    second = jnp.concatenate([w_out.T, w_gate, w_maps[:, STATE:]], 1)
    near = lax.all_to_all(first, ("y_lo", "z_pair"), 0, 0, tiled=True)
    before = shifted(layer_input[rows - HALO :], 1)
    after = shifted(layer_input[:HALO], -1)
    extended = jnp.concatenate([before, layer_input, after])
    extended = jnp.stack([extended, lax.ppermute(extended, "y_hi", [(0, 1), (1, 0)])])
    second_y = around(second, "y_lo")
    near, second_y, extended = together(near, second_y, extended)
    second_z = lax.all_gather(second_y, Z)
    left, right = neighbours(near)
    blocks = copies(extended, "x")
    first_pieces = (near, left, right, swapped(near), swapped(left), swapped(right))
    places = 2 * width // 16
    front_small = jnp.concatenate(
        [jnp.concatenate([conv_input, conv_maps[:, :STATE]], 1)]
        + [jnp.pad(value, (0, width + STATE - heads))[None] for value in (step_bias, decay_log)]
    )
    back_small = jnp.concatenate(
        [
            jnp.pad(conv_maps[:, STATE:], ((0, 0), (0, width - STATE))),
            jnp.repeat(skip_gain, HEAD_DIM)[None],
            norm_gain[None],
            jnp.pad(decay_log, (0, width - heads))[None],
        ]
    )
    send, stream, conv, step = kernel_call(
        front_kernel,
        (
            struct((places, 24, STATE), BF16),
            struct((2 * EXT, 8 * features), BF16),
            struct((2, SPAN, width + STATE), BF16),
            struct((2, SPAN, 128), F32),
        ),
        [pltpu.VMEM((2 * EXT, width + STATE), F32), pltpu.VMEM((8 * features, width + 2 * STATE), BF16)],
        [smem] + [vmem] * 8,
    )(
        place, blocks, *first_pieces, front_small,
    )
    got = lax.all_to_all(send, SEQ, 0, 0, tiled=True)
    second_own, got = together(second_z, got)
    second_other = swapped(second_own)
    entries = kernel_call(scan_kernel, struct((places, 16, STATE), BF16), [], [smem, vmem])(place, got)
    entry = lax.all_to_all(entries, SEQ, 0, 0, tiled=True).reshape(2 * width, STATE)
    out_map, inner, gate, weights = kernel_call(
        inner_kernel,
        (
            struct((2, SPAN, STATE), BF16),
            struct((2, SPAN, width), F32),
            struct((2, SPAN, width), F32),
            struct((2, 8 * features, width), BF16),
        ),
        [pltpu.VMEM((2 * EXT, STATE), F32), pltpu.VMEM((8 * features, width + STATE), BF16)],
        [smem] + [vmem] * 6,
    )(place, stream, second_own, second_other, conv, step, back_small)
    partial = kernel_call(out_kernel, struct((4, 2, SPAN, features), BF16), [])(
        entry, out_map, inner, gate, weights, back_small
    )
    parts = jnp.sum(lax.all_to_all(partial, "x", 0, 0, tiled=True).astype(F32), 0)
    low = lax.axis_index("y_hi") == 0
    kept, sent = jnp.where(low, parts[0], parts[1]), jnp.where(low, parts[1], parts[0]).astype(BF16)
    return (kept + lax.ppermute(sent, "y_hi", [(0, 1), (1, 0)]).astype(F32)).astype(BF16)


def solution(mesh):
    fine = Mesh(mesh.devices.reshape(4, 4, 2, 2, 2, 4), AXES)
    placed = (
        P(SEQ, HEAD), P(SEQ, HEAD), P(SEQ, HEAD), P(SEQ, None), P(SEQ, HEAD), P(HEAD), P(HEAD), P(HEAD), P(None, HEAD), P(), P(HEAD), P(HEAD, SEQ),
    )
    return jax.shard_map(local, mesh=fine, in_specs=placed, out_specs=P(SEQ, HEAD), check_vma=False)
```

```python
import jax
import jax.numpy as jnp
from jax import lax
from jax.experimental import pallas as pl
from jax.experimental.pallas import tpu as pltpu
from jax.sharding import Mesh
from jax.sharding import PartitionSpec as P

HEAD_DIM = 64
SPAN = 128
CONV = 4
STATE = 128
HALO = 16
EXT = SPAN + HALO
AXES = ("y_pair", "y_bit", "z", "core", "y_hi", "x")
SEQ = ("y_pair", "y_bit", "z", "core")
Y_LO = ("y_pair", "y_bit")
HEAD = ("y_hi", "x")
F32 = jnp.float32
BF16 = jnp.bfloat16


def iota(shape, axis):
    return lax.broadcasted_iota(jnp.int32, shape, axis)


def ones_where(mask):
    return jnp.where(mask, 1.0, 0.0).astype(BF16)


def mm(a, b):
    return jnp.dot(a, b, preferred_element_type=F32)


def mm_t(a, b):
    return lax.dot_general(a, b, (((1,), (1,)), ((), ())), preferred_element_type=F32)


def t_mm(a, b):
    return lax.dot_general(a, b, (((0,), (0,)), ((), ())), preferred_element_type=F32)


def split(value, parts):
    pieces = []
    for _ in range(parts):
        piece = value.astype(BF16)
        pieces.append(piece)
        value = value - piece.astype(F32)
    return pieces


def silu(value):
    return value * (1.0 / (1.0 + jnp.exp(-value)))


def reversal(size):
    return ones_where(iota((size, size), 0) + iota((size, size), 1) == size - 1)


def spread(value, width):
    table = ones_where(iota((128, width), 0) == iota((128, width), 1) // HEAD_DIM)
    return sum(mm(piece, table) for piece in split(value, 2))


def running_sum(rate):
    lower = ones_where(iota((SPAN, SPAN), 0) >= iota((SPAN, SPAN), 1))
    return sum(mm(lower, piece) for piece in split(rate, 3))


def assemble(place_ref, pieces, full_ref):
    bit, core = place_ref[1], place_ref[2]
    for side in range(2):
        near, far = pieces[2 * side : 2 * side + 2]
        column = core + side - 2 * core * side
        for block in range(16):
            start = 1024 * (block // 8) + 64 * (block % 8) + 32 * column
            full_ref[pl.ds(pl.multiple_of(start + 512 * bit, 32), 32)] = near[block]
            full_ref[pl.ds(pl.multiple_of(start + 512 * (1 - bit), 32), 32)] = far[block]


def pack_kernel(input_ref, maps_ref, step_ref, out_ref):
    heads = step_ref.shape[0]
    step = t_mm(step_ref[...], ones_where(iota((heads, 128), 0) == iota((heads, 128), 1))).astype(BF16)
    block = jnp.concatenate([input_ref[...], maps_ref[:, :STATE], step], 1)
    for copy in range(out_ref.shape[0]):
        out_ref[copy] = block


def front_kernel(
    place_ref, x_ref, n0, f0, n1, f1, small_ref,
    send_ref, stream_ref, conv_ref, step_ref, rows_ref, full_ref,
):
    assemble(place_ref, (n0, f0, n1, f1), full_ref)
    y_hi = place_ref[4]
    flip_rows, flip_columns = reversal(EXT), reversal(256)
    for step in range(4):
        for side in range(2):
            block = 4 * (y_hi + side - 2 * y_hi * side) + step
            stream_ref[:EXT, pl.ds(pl.multiple_of(block * 256, 256), 256)] = x_ref[step, side, :EXT]
            turned = mm(x_ref[step, side, HALO:], flip_columns).astype(BF16)
            stream_ref[EXT:, pl.ds(pl.multiple_of((7 - block) * 256, 256), 256)] = mm(flip_rows, turned).astype(BF16)
    proj = mm(stream_ref[...], full_ref[...])
    conv_width = conv_ref.shape[2]
    taps, bias, decay = small_ref[:CONV], small_ref[4:5, :128], small_ref[5:6, :128]
    rows_ref[...] = proj[:, :conv_width].astype(BF16).astype(F32)
    for branch in range(2):
        base = branch * EXT + HALO - (CONV - 1)
        running = taps[0:1] * rows_ref[base : base + SPAN]
        for tap in range(1, CONV):
            running = running + taps[tap : tap + 1] * rows_ref[base + tap : base + tap + SPAN]
        convolved = silu(running).astype(BF16)
        conv_ref[branch] = convolved
        raw = proj[branch * EXT + HALO : (branch + 1) * EXT, conv_width:] + bias
        step = jnp.maximum(raw, 0.0) + jnp.log1p(jnp.exp(-jnp.abs(raw)))
        cum = running_sum(step * -jnp.exp(decay))
        step_ref[branch] = step
        end = cum[SPAN - 1 : SPAN]
        x_width = conv_width - STATE
        weighted = (
            convolved[:, :x_width].astype(F32) * spread(jnp.exp(end - cum) * step, x_width)
        ).astype(BF16)
        state = t_mm(weighted, convolved[:, x_width:])
        high, low = (piece.astype(F32) for piece in split(jnp.exp(end), 2))
        row = iota((8, 128), 0)
        tiles = []
        for head in range(x_width // HEAD_DIM):
            tile = jnp.where(row == 0, high[:, head : head + 1], jnp.where(row == 1, low[:, head : head + 1], 0.0))
            tiles += [tile[None]] * 4
        count = x_width // 16
        send_ref[branch * count : (branch + 1) * count] = jnp.concatenate(
            [state.reshape(count, 16, STATE), jnp.concatenate(tiles, 0)], 1
        ).astype(BF16)


def scan_kernel(place_ref, got_ref, entry_ref):
    blocks = got_ref.shape[0]
    backward = jnp.where(place_ref[0] >= blocks // 2, 1, 0)

    def one(lap, state):
        block = lap + backward * (blocks - 1 - 2 * lap)
        entry_ref[block] = state.astype(BF16)
        got = got_ref[block].astype(F32)
        return state * (got[16:17] + got[17:18]) + got[:16]

    lax.fori_loop(0, blocks, one, jnp.zeros((16, STATE), F32), unroll=4)


def order(place_ref, pieces, columns, full_ref):
    core, y_lo = place_ref[2], place_ref[3]
    for side, ref in enumerate(pieces):
        column = core + side - 2 * core * side
        for step in range(4):
            y = (y_lo + 4 - step) % 4
            for z in range(8):
                start = 512 * y + 64 * z + 32 * column
                full_ref[pl.ds(pl.multiple_of(start, 32), 32)] = ref[z, step, :, columns]


def inner_kernel(
    place_ref, stream_ref, own_ref, other_ref, conv_ref, step_ref, small_ref,
    map_ref, inner_ref, gate_ref, weights_ref, rows_ref, full_ref,
):
    width = inner_ref.shape[2]
    order(place_ref, (own_ref, other_ref), slice(0, width), weights_ref)
    order(place_ref, (own_ref, other_ref), slice(width, width + width + STATE), full_ref)
    proj = mm(stream_ref[...], full_ref[...])
    taps, log_rate = small_ref[:CONV, :STATE], small_ref[6:7, :128]
    rows_ref[...] = proj[:, width:].astype(BF16).astype(F32)
    causal = iota((SPAN, SPAN), 0) >= iota((SPAN, SPAN), 1)
    for branch in range(2):
        gate = silu(proj[branch * EXT + HALO : (branch + 1) * EXT, :width].astype(BF16).astype(F32))
        base = branch * EXT + HALO - (CONV - 1)
        running = taps[0:1] * rows_ref[base : base + SPAN]
        for tap in range(1, CONV):
            running = running + taps[tap : tap + 1] * rows_ref[base + tap : base + tap + SPAN]
        out_map = silu(running).astype(BF16)
        map_ref[branch] = out_map
        scores = mm_t(out_map, conv_ref[branch, :, width:])
        step = step_ref[branch]
        cum = running_sum(step * -jnp.exp(log_rate))
        cum_t, step_t = cum.T, step.T
        for head in range(width // HEAD_DIM):
            channels = slice(head * HEAD_DIM, (head + 1) * HEAD_DIM)
            differ = cum[:, head : head + 1] - cum_t[head : head + 1]
            decay = jnp.where(causal, jnp.exp(jnp.where(causal, differ, 0.0)), 0.0)
            weights = (scores * decay * step_t[head : head + 1]).astype(BF16)
            x_head = conv_ref[branch, :, channels]
            inner_ref[branch, :, channels] = mm(weights, x_head) + small_ref[4:5, channels] * x_head.astype(F32)
        inner_ref[branch] = inner_ref[branch] * gate
        gate_ref[branch] = spread(jnp.exp(cum), width) * gate


def out_kernel(
    entry_ref, map_ref, inner_in, gate_in, weights_in, small_ref, out_ref, inner_ref, gate_ref, weights_ref, sems
):
    inner_copy, gate_copy, weights_copy = (
        pltpu.make_async_copy(source, target, sems.at[place])
        for place, (source, target) in enumerate(
            ((inner_in, inner_ref), (gate_in, gate_ref), (weights_in, weights_ref))
        )
    )
    for copy in (inner_copy, gate_copy, weights_copy):
        copy.start()
    width = inner_ref.shape[2]
    carried_in = [
        mm_t(map_ref[branch], entry_ref[branch * width : (branch + 1) * width]) for branch in range(2)
    ]
    inner_copy.wait()
    gate_copy.wait()
    normed = []
    for branch, carried in enumerate(carried_in):
        gated = inner_ref[branch] + carried * gate_ref[branch]
        square = jnp.mean(gated * gated, axis=-1, keepdims=True)
        normed.append((gated * lax.rsqrt(square + 1e-05) * small_ref[5:6]).astype(BF16))
    forward, mirror = normed[0], mm(reversal(SPAN), normed[1]).astype(BF16)
    weights_copy.wait()
    flip = reversal(256)
    for block in range(8):
        near, far = (slice(part * 256, (part + 1) * 256) for part in (block, 7 - block))
        turned = mm(flip, weights_ref[far]).astype(BF16)
        out_ref[block % 4, block // 4] = (mm_t(forward, weights_ref[near]) + mm_t(mirror, turned)).astype(BF16)


def kernel_call(body, outs, scratch, in_specs=None, limit=20):
    extra = {} if in_specs is None else {"in_specs": in_specs}
    return pl.pallas_call(
        body,
        out_shape=outs,
        scratch_shapes=scratch,
        compiler_params=pltpu.CompilerParams(vmem_limit_bytes=limit << 20),
        **extra,
    )


def copies(block, axis):
    count = lax.axis_size(axis)
    return lax.all_to_all(jnp.broadcast_to(block[None], (count, *block.shape)), axis, 0, 0, tiled=True)


def shifted(value, steps):
    count = lax.axis_size(SEQ)
    route = [(source, source + steps) for source in range(count) if 0 <= source + steps < count]
    return lax.ppermute(value, SEQ, route)


def swapped(block):
    return lax.ppermute(block, "core", [(0, 1), (1, 0)])


def around(block, axis):
    count = lax.axis_size(axis)
    steps = [
        lax.ppermute(block, axis, [(place, (place + step) % count) for place in range(count)])
        for step in range(1, count)
    ]
    return jnp.stack([block, *steps])


def together(*values):
    return lax.optimization_barrier(values)


def local(
    layer_input, w_input, w_gate, w_maps, w_step, step_bias, decay_log, skip_gain, conv_input, conv_maps, norm_gain, w_out,
):
    rows, features = layer_input.shape
    width, heads = w_input.shape[1], w_step.shape[1]
    wide = 128 - heads
    place = jnp.stack([lax.axis_index(SEQ), lax.axis_index("y_bit"), lax.axis_index("core")] + [lax.axis_index(axis) for axis in (Y_LO, "y_hi")])
    smem = pl.BlockSpec(memory_space=pltpu.SMEM)
    vmem = pl.BlockSpec(memory_space=pltpu.VMEM)
    struct = jax.ShapeDtypeStruct
    first = kernel_call(pack_kernel, struct((16, w_input.shape[0], width + 2 * STATE), BF16), [])(
        w_input, w_maps, w_step.T
    )
    second = jnp.concatenate([w_out.T, w_gate, w_maps[:, STATE:]], 1)
    near = lax.all_to_all(first, ("y_pair", "z"), 0, 0, tiled=True)
    before = shifted(layer_input[rows - HALO :], 1)
    after = shifted(layer_input[:HALO], -1)
    extended = jnp.concatenate([before, layer_input, after])
    extended = jnp.stack([extended, lax.ppermute(extended, "y_hi", [(0, 1), (1, 0)])])
    second_y = around(second, Y_LO)
    near, second_y, extended = together(near, second_y, extended)
    second_z = lax.all_gather(second_y, "z")
    far = lax.ppermute(near, "y_bit", [(0, 1), (1, 0)])
    blocks = copies(extended, "x")
    far, blocks = together(far, blocks)
    first_pieces = (near, far, swapped(near), swapped(far))
    places = 2 * width // 16
    front_small = jnp.concatenate(
        [jnp.concatenate([conv_input, conv_maps[:, :STATE]], 1)]
        + [jnp.pad(value, (0, width + STATE - heads))[None] for value in (step_bias, decay_log)]
    )
    back_small = jnp.concatenate(
        [
            jnp.pad(conv_maps[:, STATE:], ((0, 0), (0, width - STATE))),
            jnp.repeat(skip_gain, HEAD_DIM)[None],
            norm_gain[None],
            jnp.pad(decay_log, (0, width - heads))[None],
        ]
    )
    send, stream, conv, step = kernel_call(
        front_kernel,
        (
            struct((places, 24, STATE), BF16),
            struct((2 * EXT, 8 * features), BF16),
            struct((2, SPAN, width + STATE), BF16),
            struct((2, SPAN, 128), F32),
        ),
        [pltpu.VMEM((2 * EXT, width + STATE), F32), pltpu.VMEM((8 * features, width + 2 * STATE), BF16)],
        [smem] + [vmem] * 6,
    )(
        place, blocks, *first_pieces, front_small,
    )
    got = lax.all_to_all(send, SEQ, 0, 0, tiled=True)
    second_own, got = together(second_z, got)
    second_other = swapped(second_own)
    entries = kernel_call(scan_kernel, struct((places, 16, STATE), BF16), [], [smem, vmem])(place, got)
    entry = lax.all_to_all(entries, SEQ, 0, 0, tiled=True).reshape(2 * width, STATE)
    out_map, inner, gate, weights = kernel_call(
        inner_kernel,
        (
            struct((2, SPAN, STATE), BF16),
            struct((2, SPAN, width), F32),
            struct((2, SPAN, width), F32),
            struct((8 * features, width), BF16),
        ),
        [pltpu.VMEM((2 * EXT, STATE), F32), pltpu.VMEM((8 * features, width + STATE), BF16)],
        [smem] + [vmem] * 6,
        60,
    )(place, stream, second_own, second_other, conv, step, back_small)
    hbm = pl.BlockSpec(memory_space=pltpu.HBM)
    partial = kernel_call(
        out_kernel,
        struct((4, 2, SPAN, features), BF16),
        [
            pltpu.VMEM((2, SPAN, width), F32),
            pltpu.VMEM((2, SPAN, width), F32),
            pltpu.VMEM((8 * features, width), BF16),
            pltpu.SemaphoreType.DMA((3,)),
        ],
        [vmem, vmem, hbm, hbm, hbm, vmem],
        60,
    )(entry, out_map, inner, gate, weights, back_small)
    parts = jnp.sum(lax.all_to_all(partial, "x", 0, 0, tiled=True).astype(F32), 0)
    low = lax.axis_index("y_hi") == 0
    kept, sent = jnp.where(low, parts[0], parts[1]), jnp.where(low, parts[1], parts[0]).astype(BF16)
    return (kept + lax.ppermute(sent, "y_hi", [(0, 1), (1, 0)]).astype(F32)).astype(BF16)


def solution(mesh):
    fine = Mesh(mesh.devices.reshape(2, 2, 8, 2, 2, 4), AXES)
    placed = (
        P(SEQ, HEAD), P(SEQ, HEAD), P(SEQ, HEAD), P(SEQ, None), P(SEQ, HEAD), P(HEAD), P(HEAD), P(HEAD), P(None, HEAD), P(), P(HEAD), P(HEAD, SEQ),
    )
    return jax.shard_map(local, mesh=fine, in_specs=placed, out_specs=P(SEQ, HEAD), check_vma=False)
```

```python
import jax
import jax.numpy as jnp
from jax import lax
from jax.experimental import pallas as pl
from jax.experimental.pallas import tpu as pltpu
from jax.sharding import Mesh
from jax.sharding import PartitionSpec as P

HEAD_DIM = 64
SPAN = 128
CONV = 4
STATE = 128
HALO = 16
EXT = SPAN + HALO
AXES = ("y_lo", "z_pair", "z_bit", "core", "y_hi", "x")
SEQ = ("y_lo", "z_pair", "z_bit", "core")
Z = ("z_pair", "z_bit")
HEAD = ("y_hi", "x")
F32 = jnp.float32
BF16 = jnp.bfloat16


def iota(shape, axis):
    return lax.broadcasted_iota(jnp.int32, shape, axis)


def ones_where(mask):
    return jnp.where(mask, 1.0, 0.0).astype(BF16)


def mm(a, b):
    return jnp.dot(a, b, preferred_element_type=F32)


def mm_t(a, b):
    return lax.dot_general(a, b, (((1,), (1,)), ((), ())), preferred_element_type=F32)


def t_mm(a, b):
    return lax.dot_general(a, b, (((0,), (0,)), ((), ())), preferred_element_type=F32)


def split(value, parts):
    pieces = []
    for _ in range(parts):
        piece = value.astype(BF16)
        pieces.append(piece)
        value = value - piece.astype(F32)
    return pieces


def silu(value):
    return value * (1.0 / (1.0 + jnp.exp(-value)))


def reversal(size):
    return ones_where(iota((size, size), 0) + iota((size, size), 1) == size - 1)


def spread(value, width):
    table = ones_where(iota((128, width), 0) == iota((128, width), 1) // HEAD_DIM)
    return sum(mm(piece, table) for piece in split(value, 2))


def running_sum(rate):
    lower = ones_where(iota((SPAN, SPAN), 0) >= iota((SPAN, SPAN), 1))
    return sum(mm(lower, piece) for piece in split(rate, 3))


def assemble(place_ref, pieces, full_ref):
    bit, core = place_ref[1], place_ref[2]
    for side in range(2):
        near, left, right = pieces[3 * side : 3 * side + 3]
        column = core + side - 2 * core * side
        for block in range(16):
            far = left.at[block] if block < 8 else right.at[block - 8]
            start = 128 * block + 32 * column
            full_ref[pl.ds(pl.multiple_of(start + 64 * bit, 32), 32)] = near[block]
            full_ref[pl.ds(pl.multiple_of(start + 64 * (1 - bit), 32), 32)] = far[...]


def pack_kernel(input_ref, maps_ref, step_ref, out_ref):
    heads = step_ref.shape[0]
    step = t_mm(step_ref[...], ones_where(iota((heads, 128), 0) == iota((heads, 128), 1))).astype(BF16)
    block = jnp.concatenate([input_ref[...], maps_ref[:, :STATE], step], 1)
    for copy in range(out_ref.shape[0]):
        out_ref[copy] = block


def front_kernel(
    place_ref, x_ref, n0, l0, r0, n1, l1, r1, small_ref,
    send_ref, stream_ref, conv_ref, step_ref, rows_ref, full_ref,
):
    assemble(place_ref, (n0, l0, r0, n1, l1, r1), full_ref)
    y_hi = place_ref[4]
    flip_rows, flip_columns = reversal(EXT), reversal(256)
    for step in range(4):
        for side in range(2):
            block = 4 * (y_hi + side - 2 * y_hi * side) + step
            stream_ref[:EXT, pl.ds(pl.multiple_of(block * 256, 256), 256)] = x_ref[step, side, :EXT]
            turned = mm(x_ref[step, side, HALO:], flip_columns).astype(BF16)
            stream_ref[EXT:, pl.ds(pl.multiple_of((7 - block) * 256, 256), 256)] = mm(flip_rows, turned).astype(BF16)
    proj = mm(stream_ref[...], full_ref[...])
    conv_width = conv_ref.shape[2]
    taps, bias, decay = small_ref[:CONV], small_ref[4:5, :128], small_ref[5:6, :128]
    rows_ref[...] = proj[:, :conv_width].astype(BF16).astype(F32)
    for branch in range(2):
        base = branch * EXT + HALO - (CONV - 1)
        running = taps[0:1] * rows_ref[base : base + SPAN]
        for tap in range(1, CONV):
            running = running + taps[tap : tap + 1] * rows_ref[base + tap : base + tap + SPAN]
        convolved = silu(running).astype(BF16)
        conv_ref[branch] = convolved
        raw = proj[branch * EXT + HALO : (branch + 1) * EXT, conv_width:] + bias
        step = jnp.maximum(raw, 0.0) + jnp.log1p(jnp.exp(-jnp.abs(raw)))
        cum = running_sum(step * -jnp.exp(decay))
        step_ref[branch] = step
        end = cum[SPAN - 1 : SPAN]
        x_width = conv_width - STATE
        weighted = (
            convolved[:, :x_width].astype(F32) * spread(jnp.exp(end - cum) * step, x_width)
        ).astype(BF16)
        state = t_mm(weighted, convolved[:, x_width:])
        high, low = (piece.astype(F32) for piece in split(jnp.exp(end), 2))
        row = iota((8, 128), 0)
        tiles = []
        for head in range(x_width // HEAD_DIM):
            tile = jnp.where(row == 0, high[:, head : head + 1], jnp.where(row == 1, low[:, head : head + 1], 0.0))
            tiles += [tile[None]] * 4
        count = x_width // 16
        send_ref[branch * count : (branch + 1) * count] = jnp.concatenate(
            [state.reshape(count, 16, STATE), jnp.concatenate(tiles, 0)], 1
        ).astype(BF16)


def scan_kernel(place_ref, got_ref, entry_ref):
    blocks = got_ref.shape[0]
    backward = jnp.where(place_ref[0] >= blocks // 2, 1, 0)

    def one(lap, state):
        block = lap + backward * (blocks - 1 - 2 * lap)
        entry_ref[block] = state.astype(BF16)
        got = got_ref[block].astype(F32)
        return state * (got[16:17] + got[17:18]) + got[:16]

    lax.fori_loop(0, blocks, one, jnp.zeros((16, STATE), F32), unroll=4)


def order(place_ref, pieces, columns, full_ref):
    core, y_lo = place_ref[2], place_ref[3]
    for side, ref in enumerate(pieces):
        column = core + side - 2 * core * side
        for step in range(4):
            y = (y_lo + 4 - step) % 4
            for z in range(8):
                start = 512 * y + 64 * z + 32 * column
                full_ref[pl.ds(pl.multiple_of(start, 32), 32)] = ref[z, step, :, columns]


def inner_kernel(
    place_ref, stream_ref, own_ref, other_ref, conv_ref, step_ref, small_ref,
    map_ref, inner_ref, gate_ref, weights_ref, rows_ref, full_ref,
):
    width = inner_ref.shape[2]
    order(place_ref, (own_ref, other_ref), slice(0, width), weights_ref)
    order(place_ref, (own_ref, other_ref), slice(width, width + width + STATE), full_ref)
    proj = mm(stream_ref[...], full_ref[...])
    taps, log_rate = small_ref[:CONV, :STATE], small_ref[6:7, :128]
    rows_ref[...] = proj[:, width:].astype(BF16).astype(F32)
    causal = iota((SPAN, SPAN), 0) >= iota((SPAN, SPAN), 1)
    for branch in range(2):
        gate = silu(proj[branch * EXT + HALO : (branch + 1) * EXT, :width].astype(BF16).astype(F32))
        base = branch * EXT + HALO - (CONV - 1)
        running = taps[0:1] * rows_ref[base : base + SPAN]
        for tap in range(1, CONV):
            running = running + taps[tap : tap + 1] * rows_ref[base + tap : base + tap + SPAN]
        out_map = silu(running).astype(BF16)
        map_ref[branch] = out_map
        scores = mm_t(out_map, conv_ref[branch, :, width:])
        step = step_ref[branch]
        cum = running_sum(step * -jnp.exp(log_rate))
        cum_t, step_t = cum.T, step.T
        for head in range(width // HEAD_DIM):
            channels = slice(head * HEAD_DIM, (head + 1) * HEAD_DIM)
            differ = cum[:, head : head + 1] - cum_t[head : head + 1]
            decay = jnp.where(causal, jnp.exp(jnp.where(causal, differ, 0.0)), 0.0)
            weights = (scores * decay * step_t[head : head + 1]).astype(BF16)
            x_head = conv_ref[branch, :, channels]
            inner_ref[branch, :, channels] = mm(weights, x_head) + small_ref[4:5, channels] * x_head.astype(F32)
        inner_ref[branch] = inner_ref[branch] * gate
        gate_ref[branch] = spread(jnp.exp(cum), width) * gate


def out_kernel(
    entry_ref, map_ref, inner_in, gate_in, weights_in, small_ref, out_ref, inner_ref, gate_ref, weights_ref, sems
):
    inner_copy, gate_copy, weights_copy = (
        pltpu.make_async_copy(source, target, sems.at[place])
        for place, (source, target) in enumerate(
            ((inner_in, inner_ref), (gate_in, gate_ref), (weights_in, weights_ref))
        )
    )
    for copy in (inner_copy, gate_copy, weights_copy):
        copy.start()
    width = inner_ref.shape[2]
    carried_in = [
        mm_t(map_ref[branch], entry_ref[branch * width : (branch + 1) * width]) for branch in range(2)
    ]
    inner_copy.wait()
    gate_copy.wait()
    normed = []
    for branch, carried in enumerate(carried_in):
        gated = inner_ref[branch] + carried * gate_ref[branch]
        square = jnp.mean(gated * gated, axis=-1, keepdims=True)
        normed.append((gated * lax.rsqrt(square + 1e-05) * small_ref[5:6]).astype(BF16))
    forward, mirror = normed[0], mm(reversal(SPAN), normed[1]).astype(BF16)
    weights_copy.wait()
    flip = reversal(256)
    for block in range(8):
        near, far = (slice(part * 256, (part + 1) * 256) for part in (block, 7 - block))
        turned = mm(flip, weights_ref[far]).astype(BF16)
        out_ref[block % 4, block // 4] = (mm_t(forward, weights_ref[near]) + mm_t(mirror, turned)).astype(BF16)


def kernel_call(body, outs, scratch, in_specs=None, limit=20):
    extra = {} if in_specs is None else {"in_specs": in_specs}
    return pl.pallas_call(
        body,
        out_shape=outs,
        scratch_shapes=scratch,
        compiler_params=pltpu.CompilerParams(vmem_limit_bytes=limit << 20),
        **extra,
    )


def copies(block, axis):
    count = lax.axis_size(axis)
    return lax.all_to_all(jnp.broadcast_to(block[None], (count, *block.shape)), axis, 0, 0, tiled=True)


def shifted(value, steps):
    count = lax.axis_size(SEQ)
    route = [(source, source + steps) for source in range(count) if 0 <= source + steps < count]
    return lax.ppermute(value, SEQ, route)


def swapped(block):
    return lax.ppermute(block, "core", [(0, 1), (1, 0)])


def neighbours(near):
    count, half = lax.axis_size(Z), near.shape[0] // 2
    left = lax.ppermute(near[:half], Z, [(z, (z + 1) % count) for z in range(count)])
    right = lax.ppermute(near[half:], Z, [(z, (z - 1) % count) for z in range(count)])
    return left, right


def around(block, axis):
    count = lax.axis_size(axis)
    steps = [
        lax.ppermute(block, axis, [(place, (place + step) % count) for place in range(count)])
        for step in range(1, count)
    ]
    return jnp.stack([block, *steps])


def together(*values):
    return lax.optimization_barrier(values)


def local(
    layer_input, w_input, w_gate, w_maps, w_step, step_bias, decay_log, skip_gain, conv_input, conv_maps, norm_gain, w_out,
):
    rows, features = layer_input.shape
    width, heads = w_input.shape[1], w_step.shape[1]
    wide = 128 - heads
    place = jnp.stack([lax.axis_index(SEQ), lax.axis_index("z_bit"), lax.axis_index("core")] + [lax.axis_index(axis) for axis in ("y_lo", "y_hi")])
    smem = pl.BlockSpec(memory_space=pltpu.SMEM)
    vmem = pl.BlockSpec(memory_space=pltpu.VMEM)
    struct = jax.ShapeDtypeStruct
    first = kernel_call(pack_kernel, struct((16, w_input.shape[0], width + 2 * STATE), BF16), [])(
        w_input, w_maps, w_step.T
    )
    second = jnp.concatenate([w_out.T, w_gate, w_maps[:, STATE:]], 1)
    near = lax.all_to_all(first, ("y_lo", "z_pair"), 0, 0, tiled=True)
    before = shifted(layer_input[rows - HALO :], 1)
    after = shifted(layer_input[:HALO], -1)
    extended = jnp.concatenate([before, layer_input, after])
    extended = jnp.stack([extended, lax.ppermute(extended, "y_hi", [(0, 1), (1, 0)])])
    second_y = around(second, "y_lo")
    near, second_y, extended = together(near, second_y, extended)
    second_z = lax.all_gather(second_y, Z)
    left, right = neighbours(near)
    blocks = copies(extended, "x")
    first_pieces = (near, left, right, swapped(near), swapped(left), swapped(right))
    places = 2 * width // 16
    front_small = jnp.concatenate(
        [jnp.concatenate([conv_input, conv_maps[:, :STATE]], 1)]
        + [jnp.pad(value, (0, width + STATE - heads))[None] for value in (step_bias, decay_log)]
    )
    back_small = jnp.concatenate(
        [
            jnp.pad(conv_maps[:, STATE:], ((0, 0), (0, width - STATE))),
            jnp.repeat(skip_gain, HEAD_DIM)[None],
            norm_gain[None],
            jnp.pad(decay_log, (0, width - heads))[None],
        ]
    )
    send, stream, conv, step = kernel_call(
        front_kernel,
        (
            struct((places, 24, STATE), BF16),
            struct((2 * EXT, 8 * features), BF16),
            struct((2, SPAN, width + STATE), BF16),
            struct((2, SPAN, 128), F32),
        ),
        [pltpu.VMEM((2 * EXT, width + STATE), F32), pltpu.VMEM((8 * features, width + 2 * STATE), BF16)],
        [smem] + [vmem] * 8,
    )(
        place, blocks, *first_pieces, front_small,
    )
    got = lax.all_to_all(send, SEQ, 0, 0, tiled=True)
    second_own, got = together(second_z, got)
    second_other = swapped(second_own)
    entries = kernel_call(scan_kernel, struct((places, 16, STATE), BF16), [], [smem, vmem])(place, got)
    entry = lax.all_to_all(entries, SEQ, 0, 0, tiled=True).reshape(2 * width, STATE)
    out_map, inner, gate, weights = kernel_call(
        inner_kernel,
        (
            struct((2, SPAN, STATE), BF16),
            struct((2, SPAN, width), F32),
            struct((2, SPAN, width), F32),
            struct((8 * features, width), BF16),
        ),
        [pltpu.VMEM((2 * EXT, STATE), F32), pltpu.VMEM((8 * features, width + STATE), BF16)],
        [smem] + [vmem] * 6,
        60,
    )(place, stream, second_own, second_other, conv, step, back_small)
    hbm = pl.BlockSpec(memory_space=pltpu.HBM)
    partial = kernel_call(
        out_kernel,
        struct((4, 2, SPAN, features), BF16),
        [
            pltpu.VMEM((2, SPAN, width), F32),
            pltpu.VMEM((2, SPAN, width), F32),
            pltpu.VMEM((8 * features, width), BF16),
            pltpu.SemaphoreType.DMA((3,)),
        ],
        [vmem, vmem, hbm, hbm, hbm, vmem],
        60,
    )(entry, out_map, inner, gate, weights, back_small)
    parts = jnp.sum(lax.all_to_all(partial, "x", 0, 0, tiled=True).astype(F32), 0)
    low = lax.axis_index("y_hi") == 0
    kept, sent = jnp.where(low, parts[0], parts[1]), jnp.where(low, parts[1], parts[0]).astype(BF16)
    return (kept + lax.ppermute(sent, "y_hi", [(0, 1), (1, 0)]).astype(F32)).astype(BF16)


def solution(mesh):
    fine = Mesh(mesh.devices.reshape(4, 4, 2, 2, 2, 4), AXES)
    placed = (
        P(SEQ, HEAD), P(SEQ, HEAD), P(SEQ, HEAD), P(SEQ, None), P(SEQ, HEAD), P(HEAD), P(HEAD), P(HEAD), P(None, HEAD), P(), P(HEAD), P(HEAD, SEQ),
    )
    return jax.shard_map(local, mesh=fine, in_specs=placed, out_specs=P(SEQ, HEAD), check_vma=False)
```
